1024 devices in a mesh: dp: 8 (over x), context: 16 (over y, core), tensor: 8 (over z).
Axes of the slice: x: 8, y: 8, z: 8, core: 2. Of those that a mesh axis runs over, the one named last changes fastest.
Arguments:
- hidden: bfloat16 [32768, 4096], P(('dp', 'context')), parts along dimension 0, may hold values from -6 to 6
- expert_ids: int32 [32768, 8], P(('dp', 'context')), parts along dimension 0, may hold values from 0 to 127, all different within a row; in each aligned block of 256 rows (0 to 255, 256 to 511, ...) at most 32 rows name the same one
- gate_weights: float32 [32768, 8], P(('dp', 'context')), parts along dimension 0, may hold values from 0.2 to 1
- w_gate: bfloat16 [16, 4096, 1536], P('context', None, 'tensor'), may hold values from -0.09375 to 0.09375
- w_up: bfloat16 [16, 4096, 1536], P('context', None, 'tensor'), may hold values from -0.09375 to 0.09375
- w_down: bfloat16 [16, 1536, 4096], P('context', 'tensor'), may hold values from -0.21875 to 0.21875
Outputs:
- mixed: bfloat16 [32768, 4096], P(('dp', 'context'), 'tensor'), parts along dimension 0
The draws below stay inside these ranges and needn't reach their ends.
There are 8 independent parts, one for each index of `dp`. The reference program is written for one: setup_inputs(seed, part) draws one part's arguments, and reference() takes and returns one part's arrays. A program takes and returns all parts, laid end to end along the dimension named above; an argument that names none is the same for every part. Nothing has to cross between parts.
Inputs may be any that keep to these rules, and one draw needn't show every extreme that they name: `expert_ids`: each row names 8 different experts. Among the 256 rows of one context index no expert is named by more than 32 rows, a bound that some block reaches.
All inputs are finite; a program needn't handle non-finite values.
Results may differ from the reference program's by a relative error of at most 0.02.
Values may be sent and summed in bfloat16 or wider, within the bound.
A program may use at most 64 MiB of HBM per device.

```python
import math
import jax
import jax.numpy as jnp
import numpy as np
from jax import lax

D = 4096
FF = 1536
EXPERTS = 128
TOP = 8
TOK_CTX = 256
CAP = 32
LIVE = 16
TOKENS = 4096
N_CONTEXT = 16
N_TENSOR = 8


def spiked(result, own_key, source, target, blocks, factor):
    owner, partner = [(jnp.arange(result.shape[dim]) // (result.shape[dim] // blocks)).reshape([-1 if axis == dim else 1 for axis in range(result.ndim)]) for dim in (source, target)]
    chosen = jax.random.permutation(own_key, blocks)[partner]
    strong = (owner == chosen) | (owner == (partner + blocks // 2) % blocks)
    return jnp.where(strong, factor * result, result)


def level_of(key, dims, shards, least, high):
    gain = 1.0
    for axis_at, shards_of in shards:
        draws = jax.random.uniform(jax.random.fold_in(jax.random.fold_in(key, 6), axis_at), (shards_of,), jnp.float32, least / len(shards), high / len(shards))
        gain = gain * jnp.repeat(jnp.exp(draws), dims[axis_at] // shards_of).reshape((-1,) + (1,) * (len(dims) - 1 - axis_at))
    return gain


def routed_block(stream_key, own, number, rows, amount, top, most, skew):
    ranking = jax.random.permutation(stream_key, amount)
    crowded, common = portions_of(amount, rows * top, most, skew, True), portions_of(amount, rows * top, most, skew, False)
    places = jnp.arange(amount)

    def named(lengths, rotation):
        used = int((lengths > 0).sum())
        fixed = max(1, used // 4)
        moved = fixed + (places - fixed + rotation * (used - fixed)) % max(1, amount - fixed)
        return jnp.zeros((amount,), jnp.int32).at[ranking[jnp.where(places < fixed, places, moved)]].set(jnp.asarray(lengths, jnp.int32))

    lengths = jnp.where(number % 4 == 0, named(crowded, number // 4), named(common, number - number // 4 - 1))
    mixed = jax.random.permutation(jax.random.fold_in(own, 3), amount)
    donor, taker = mixed[0:amount // 2 * 2:2], mixed[1:amount // 2 * 2:2]
    margin = jnp.minimum(lengths[donor] - 1, most - lengths[taker]) // 2
    margin = jnp.where((donor == ranking[0]) | (taker == ranking[0]) | (lengths[taker] == 0), 0, jnp.maximum(margin, 0))
    moved = jax.random.randint(jax.random.fold_in(own, 4), (amount // 2,), 0, 1 << 20) % (margin + 1)
    lengths = lengths.at[donor].add(-moved).at[taker].add(moved)
    items = jnp.searchsorted(jnp.cumsum(lengths), jnp.arange(rows * top), side="right").astype(jnp.int32)
    grid = items.reshape(top, rows).T
    grid = grid[jax.random.permutation(jax.random.fold_in(own, 1), rows)]
    rotation = jax.random.randint(jax.random.fold_in(own, 2), (rows, 1), 0, top)
    return jnp.take_along_axis(grid, (jnp.arange(top)[None, :] + rotation) % top, axis=1)


def portions_of(number_of, total, reach, lean, full):
    loads = [(1 << 20) // math.isqrt(grade ** lean) + 1 for grade in range(1, number_of + 1)]
    largest = reach if full else min(reach, max(-(-total // number_of), total * loads[0] // sum(loads)))
    least = 1 if total - largest >= number_of - 1 else 0
    given, spare = [largest] + [least] * (number_of - 1), total - largest - least * (number_of - 1)
    while spare > 0:
        candidates = [i for i in range(1, number_of) if given[i] < largest] or [i for i in range(1, number_of) if given[i] < reach]
        mass, budget = sum([loads[i] for i in candidates]), spare
        for i in candidates:
            more = min(reach - given[i], max(1, budget * loads[i] // mass), spare)
            given[i] = given[i] + more
            spare = spare - more
    return np.array(given)


def gaussian(stream_key, dims, scale, most, cuts=(), held_as=jnp.bfloat16):
    values = jax.random.normal(stream_key, dims, jnp.float32) * scale
    if len(cuts) > 0:
        values = level_of(stream_key, dims, cuts, -0.22, 0.18) * values
    return jnp.clip(values, min=-most, max=most).astype(held_as)


def gaussian_with(rng, extent, scale, reach, pieces, heavy, held_as=jnp.bfloat16):
    entries = scale * jax.random.normal(rng, extent, jnp.float32)
    if pieces:
        entries = entries * level_of(rng, extent, pieces, -0.22, 0.18)
    return jnp.clip(spiked(entries, jax.random.fold_in(rng, 3), *heavy), -reach, reach).astype(held_as)


def setup_inputs(seed: int = 0, part: int = 0) -> dict:
    keys = jax.random.split(jax.random.key(seed), 7)
    part_splits = jax.random.split(jax.random.fold_in(keys[6], part), 7)
    hidden = gaussian(part_splits[0], (TOKENS, D), 1.0, 6.0, ((0, 16),))
    expert_ids_keys = jax.random.split(jax.random.fold_in(part_splits[1], 1), TOKENS // TOK_CTX)
    expert_ids_turns = jax.random.permutation(jax.random.fold_in(part_splits[1], 3), TOKENS // TOK_CTX)
    expert_ids = jax.vmap(lambda own, number: routed_block(jax.random.fold_in(part_splits[1], 2), own, number, TOK_CTX, EXPERTS, TOP, CAP, 2))(expert_ids_keys, expert_ids_turns).reshape((TOKENS, TOP))
    gate_weights = jnp.clip(0.2 + 0.8 * jax.random.uniform(part_splits[2], (TOKENS, TOP), jnp.float32) ** level_of(part_splits[2], (TOKENS, TOP), ((0, 16),), -0.2, 0.2), 0.2, 1.0)
    w_gate = gaussian(keys[3], (LIVE, D, FF), D ** -0.5, 0.09375, ((0, 16), (2, 8)))
    w_up = gaussian(keys[4], (LIVE, D, FF), D ** -0.5, 0.09375, ((0, 16), (2, 8)))
    w_down = gaussian_with(keys[5], (LIVE, FF, D), FF ** -0.5, 0.21875, ((0, 16), (1, 8)), (1, 2, 8, 2.0))
    return dict(hidden=hidden, expert_ids=expert_ids, gate_weights=gate_weights, w_gate=w_gate, w_up=w_up, w_down=w_down)


def reference(hidden, expert_ids, gate_weights, w_gate, w_up, w_down):
    positions = jnp.arange(TOKENS).astype(jnp.int32)
    block_index = positions // TOK_CTX
    slice_hidden = FF // N_TENSOR
    totals = jnp.zeros((TOKENS, D), jnp.float32)
    for expert in range(LIVE):
        matches = expert_ids == expert
        marked = jnp.any(matches, axis=1)
        weight = jnp.sum(jnp.where(matches, gate_weights, jnp.float32(0.0)), axis=1)
        counted = marked.astype(jnp.int32).reshape(N_CONTEXT, TOK_CTX)
        position = (jnp.cumsum(counted, axis=1) - 1).reshape(TOKENS).astype(jnp.int32)
        slot_index = jnp.where(marked, block_index * CAP + position, N_CONTEXT * CAP).astype(jnp.int32)
        token_index = jnp.zeros((N_CONTEXT * CAP,), jnp.int32).at[slot_index].set(positions, mode="drop")
        slot_weight = jnp.zeros((N_CONTEXT * CAP,), jnp.float32).at[slot_index].set(weight, mode="drop")
        filled = jnp.zeros((N_CONTEXT * CAP,), jnp.float32).at[slot_index].set(jnp.float32(1.0), mode="drop")
        picked = (hidden[token_index].astype(jnp.float32) * filled[:, None]).astype(jnp.bfloat16)
        gate_acts = jnp.dot(picked, w_gate[expert], preferred_element_type=jnp.float32)
        up_acts = jnp.dot(picked, w_up[expert], preferred_element_type=jnp.float32)
        activated = (jax.nn.silu(gate_acts) * up_acts).astype(jnp.bfloat16)
        act_blocks = activated.reshape(N_CONTEXT * CAP, N_TENSOR, slice_hidden).astype(jnp.float32)
        down_blocks = w_down[expert].reshape(N_TENSOR, slice_hidden, D).astype(jnp.float32)
        parts = jnp.einsum("rnf,nfd->nrd", act_blocks, down_blocks, precision=lax.Precision.HIGHEST)
        parts = lax.optimization_barrier(parts.astype(jnp.bfloat16))
        expert_out = jnp.sum(parts.astype(jnp.float32), axis=0).astype(jnp.bfloat16)
        totals = totals.at[token_index].add(slot_weight[:, None] * expert_out.astype(jnp.float32))
    return totals.astype(jnp.bfloat16)
```

```python
import jax
import jax.numpy as jnp
from jax import lax
from jax.experimental import pallas as pl
from jax.experimental.pallas import tpu as pltpu
from jax.sharding import PartitionSpec as P

CAP = 32
CHIPS = 8
OFFSETS = (0, 1, 7, 2, 6, 3, 5, 4)
CHUNKS = ((0, 1, True), (1, 2, False), (3, 2, False), (5, 2, False), (7, 1, True))
PIECES = 2
ORDER = (
    ("Y", 0), ("Y", 1), ("W",), ("Y", 2), ("Y", 3), ("Y", 4),
    ("A", 0), ("B", 0), ("S", 0, 0), ("S", 0, 1), ("A", 1), ("S", 0, 2),
    ("B", 1), ("S", 1, 0), ("S", 0, 3), ("A", 2), ("S", 1, 1), ("F", 0),
    ("B", 2), ("S", 2, 0), ("S", 1, 2), ("S", 2, 1), ("A", 3), ("S", 1, 3),
    ("S", 2, 2), ("B", 3), ("S", 3, 0), ("F", 1), ("S", 2, 3), ("S", 3, 1),
    ("F", 2), ("A", 4), ("B", 4), ("S", 4, 0), ("S", 3, 2), ("S", 4, 1),
    ("S", 3, 3), ("S", 4, 2), ("F", 3), ("S", 4, 3), ("F", 4), ("C", 0),
    ("C", 1), ("C", 2), ("C", 3), ("C", 4),
)
BOTH_LAST = (((1,), (1,)), ((), ()))
BOTH_FIRST = (((0,), (0,)), ((), ()))
MESH = pl.DeviceIdType.MESH


def kernel(
    ids_ref, mix_ref, hidden_ref, gate_ref, up_ref, down_ref, out_ref,
    sel_ref, comb_ref, total_ref, hid, wg, wu, wd, outgoing, arrived, act, rs_out, rs_in, mixed_rows, returned,
    load_sem, y_send, y_recv, f_send, f_recv, r_send, r_recv, b_send, b_recv,
):
    ctx, z = lax.axis_index("context"), lax.axis_index("tensor")
    y, core = ctx // 2, ctx % 2
    width = hidden_ref.shape[1]
    half, quarter, block = width // 2, width // 4, width // 8
    own = pl.multiple_of((z % 2) * half, half)
    other = pl.multiple_of((1 - z % 2) * half, half)
    right, left = (z + 1) % CHIPS, (z + CHIPS - 1) % CHIPS

    loads = []
    for n, (source, begin) in enumerate(((own, 0), (other, half))):
        loads.append(
            pltpu.make_async_copy(
                hidden_ref.at[:, pl.ds(source, half)], hid.at[:, pl.ds(begin, half)],
                load_sem.at[n],
            )
        )
    for n, (source, begin) in enumerate(((own, 0), (other, half))):
        for m, (src, dst) in enumerate(((gate_ref, wg), (up_ref, wu))):
            loads.append(
                pltpu.make_async_copy(
                    src.at[0, :, pl.ds(source, half)], dst.at[:, pl.ds(begin, half)],
                    load_sem.at[2 + 2 * n + m],
                )
            )
    loads.append(pltpu.make_async_copy(down_ref.at[0], wd, load_sem.at[6]))
    for load in loads:
        load.start()

    def peer(dy, dc):
        return ((y + dy) % CHIPS) * 2 + (core + dc) % 2

    barrier = pltpu.get_barrier_semaphore()
    for dy in range(CHIPS):
        for dc in range(2):
            if dy or dc:
                pl.semaphore_signal(
                    barrier, inc=1, device_id={"context": peer(dy, dc)}, device_id_type=MESH
                )
    for side in (right, left):
        pl.semaphore_signal(barrier, inc=1, device_id={"tensor": side}, device_id_type=MESH)

    tokens = hidden_ref.shape[0]
    row = lax.broadcasted_iota(jnp.int32, (2 * CHIPS, tokens), 0)
    place = row // 2
    shift = jnp.zeros_like(place)
    for n, offset in enumerate(OFFSETS):
        shift = jnp.where(place == n, offset, shift)
    expert = ((y + shift) % CHIPS) * 2 + (core + row % 2) % 2
    chosen = jnp.zeros((2 * CHIPS, tokens), jnp.float32)
    weight = jnp.zeros((2 * CHIPS, tokens), jnp.float32)
    for n in range(ids_ref.shape[0]):
        match = ids_ref[n:n + 1, :] == expert
        chosen = jnp.where(match, 1.0, chosen)
        weight = jnp.where(match, mix_ref[n:n + 1, :], weight)
    before = (
        lax.broadcasted_iota(jnp.int32, (tokens, tokens), 0)
        <= lax.broadcasted_iota(jnp.int32, (tokens, tokens), 1)
    )
    count = jnp.dot(
        chosen.astype(jnp.bfloat16), jnp.where(before, 1.0, 0.0).astype(jnp.bfloat16),
        preferred_element_type=jnp.float32,
    )
    slot = jnp.where(chosen > 0.0, count - 1.0, -1.0)
    slot_ids = lax.broadcasted_iota(jnp.int32, (CAP, tokens), 0).astype(jnp.float32)
    for n in range(2 * CHIPS):
        sel_ref[n * CAP:(n + 1) * CAP, :] = jnp.where(
            slot[n:n + 1, :] == slot_ids, 1.0, 0.0
        ).astype(jnp.bfloat16)

    loads[0].wait()
    loads[1].wait()
    pl.semaphore_wait(barrier, 2 * CHIPS + 1)

    y_copies, forwards, sums, backs = {}, {}, {}, {}

    def extent(k):
        begin, count, whole = CHUNKS[k]
        return begin * 2 * CAP, (begin + count) * 2 * CAP, 4 if whole else 2

    def dispatch(k):
        low, top, quarters = extent(k)
        for q in range(quarters):
            picked = jnp.dot(
                sel_ref[low:top, :], hid[:, q * quarter:(q + 1) * quarter],
                preferred_element_type=jnp.float32,
            ).astype(jnp.bfloat16)
            outgoing[q, low:top, :] = picked
            if low == 0:
                arrived[q, 0:CAP, :] = picked[0:CAP]
        for n in range(low // CAP, top // CAP):
            if n == 0:
                continue
            piece = (pl.ds(0, quarters), pl.ds(CAP * n, CAP), slice(None))
            copy = pltpu.make_async_remote_copy(
                src_ref=outgoing.at[piece], dst_ref=arrived.at[piece],
                send_sem=y_send.at[n], recv_sem=y_recv.at[n],
                device_id={"context": peer(OFFSETS[n // 2], n % 2)}, device_id_type=MESH,
            )
            copy.start()
            y_copies[n] = copy

    def weigh():
        for n in range(2 * CHIPS):
            combiner = jnp.where(slot[n:n + 1, :] == slot_ids, weight[n:n + 1, :], 0.0)
            high = combiner.astype(jnp.bfloat16)
            comb_ref[0, n * CAP:(n + 1) * CAP, :] = high
            comb_ref[1, n * CAP:(n + 1) * CAP, :] = (
                combiner - high.astype(jnp.float32)
            ).astype(jnp.bfloat16)

    def arrive(k):
        low, top, quarters = extent(k)
        for n in range(low // CAP, top // CAP):
            if n:
                y_copies[n].wait_recv()
        if quarters == 4:
            return
        span = pl.ds(low, top - low)
        for side, to in enumerate((right, left)):
            copy = pltpu.make_async_remote_copy(
                src_ref=arrived.at[side, span, :], dst_ref=arrived.at[2 + side, span, :],
                send_sem=f_send.at[k, side], recv_sem=f_recv.at[k, side],
                device_id={"tensor": to}, device_id_type=MESH,
            )
            copy.start()
            forwards[k, side] = copy

    def expand(k):
        low, top, quarters = extent(k)
        if k == 0:
            for load in loads[2:]:
                load.wait()
        gate = up = None
        for q in range(4):
            if q >= quarters:
                forwards[k, q - 2].wait_recv()
            x = arrived[q, low:top, :]
            here = slice(q * quarter, (q + 1) * quarter)
            g = lax.dot_general(x, wg[:, here], BOTH_LAST, preferred_element_type=jnp.float32)
            u = lax.dot_general(x, wu[:, here], BOTH_LAST, preferred_element_type=jnp.float32)
            gate = g if gate is None else gate + g
            up = u if up is None else up + u
        act[low:top, :] = (gate / (1.0 + jnp.exp(-gate)) * up).astype(jnp.bfloat16)

    def part(k, target, begin, size):
        low, top, _ = extent(k)
        columns = pl.ds(pl.multiple_of(target * block + begin, size), size)
        return jnp.dot(act[low:top, :], wd[:, columns], preferred_element_type=jnp.float32)

    narrow = block // 2

    def step(k, s):
        low, top, _ = extent(k)
        size = (top - low) // PIECES
        totals = []
        for side in range(2):
            shift = 4 - s
            target = (z + shift) % CHIPS if side == 0 else (z + CHIPS - shift) % CHIPS
            if s == 0:
                totals.append(part(k, target, side * narrow, narrow))
            else:
                totals.append(part(k, target, 0, block))
        for piece in range(PIECES):
            begin, end = low + piece * size, low + (piece + 1) * size
            for side, to in enumerate((right, left)):
                total = totals[side][piece * size:(piece + 1) * size]
                if s:
                    sums[k, s - 1, side, piece].wait_recv()
                if s == 0:
                    rs_out[side, 0, begin:end, 0:narrow] = total.astype(jnp.bfloat16)
                elif s == 1:
                    mine = slice(side * narrow, (side + 1) * narrow)
                    rest = slice((1 - side) * narrow, (2 - side) * narrow)
                    rs_out[side, s, begin:end, mine] = (
                        total[:, mine] + rs_in[side, 0, begin:end, 0:narrow].astype(jnp.float32)
                    ).astype(jnp.bfloat16)
                    rs_out[side, s, begin:end, rest] = total[:, rest].astype(jnp.bfloat16)
                else:
                    total = total + rs_in[side, s - 1, begin:end, :].astype(jnp.float32)
                    rs_out[side, s, begin:end, :] = total.astype(jnp.bfloat16)
                place = (side, s, pl.ds(begin, size), pl.ds(0, block if s else narrow))
                copy = pltpu.make_async_remote_copy(
                    src_ref=rs_out.at[place], dst_ref=rs_in.at[place],
                    send_sem=r_send.at[k, s, side, piece], recv_sem=r_recv.at[k, s, side, piece],
                    device_id={"tensor": to}, device_id_type=MESH,
                )
                copy.start()
                sums[k, s, side, piece] = copy

    def finish(k):
        low, top, _ = extent(k)
        size = (top - low) // PIECES
        whole = part(k, z, 0, block)
        for piece in range(PIECES):
            begin, end = low + piece * size, low + (piece + 1) * size
            total = whole[piece * size:(piece + 1) * size]
            for side in range(2):
                sums[k, 3, side, piece].wait_recv()
                total = total + rs_in[side, 3, begin:end, :].astype(jnp.float32)
            total = total.astype(jnp.bfloat16)
            mixed_rows[begin:end, :] = total
            for n in range(begin // CAP, end // CAP):
                if n == 0:
                    returned[0:CAP, :] = total[0:CAP]
                    continue
                span = pl.ds(CAP * n, CAP)
                copy = pltpu.make_async_remote_copy(
                    src_ref=mixed_rows.at[span, :], dst_ref=returned.at[span, :],
                    send_sem=b_send.at[n], recv_sem=b_recv.at[n],
                    device_id={"context": peer(CHIPS - OFFSETS[n // 2], n % 2)},
                    device_id_type=MESH,
                )
                copy.start()
                backs[n] = copy

    def combine(k):
        low, top, _ = extent(k)
        for n in range(low // CAP, top // CAP):
            if n:
                backs[n].wait_recv()
        total = None if k == 0 else total_ref[...]
        for n in range(2):
            term = lax.dot_general(
                comb_ref[n, low:top, :], returned[low:top, :], BOTH_FIRST,
                preferred_element_type=jnp.float32,
            )
            total = term if total is None else total + term
        if k == len(CHUNKS) - 1:
            out_ref[...] = total.astype(out_ref.dtype)
        else:
            total_ref[...] = total

    tasks = {"Y": dispatch, "A": arrive, "B": expand, "S": step, "F": finish, "C": combine, "W": weigh}
    for task in ORDER:
        tasks[task[0]](*task[1:])

    for group in (y_copies, forwards, sums, backs):
        for copy in group.values():
            copy.wait_send()


def local(hidden, expert_ids, gate_weights, w_gate, w_up, w_down):
    tokens, width = hidden.shape
    units = w_gate.shape[2]
    block = width // CHIPS
    rows = 2 * CHIPS * CAP
    chunks = len(CHUNKS)
    bf16 = jnp.bfloat16
    vmem = pl.BlockSpec(memory_space=pltpu.VMEM)
    hbm = pl.BlockSpec(memory_space=pl.ANY)
    dma = pltpu.SemaphoreType.DMA
    return pl.pallas_call(
        kernel,
        out_shape=jax.ShapeDtypeStruct((tokens, block), bf16),
        in_specs=[vmem] * 2 + [hbm] * 4,
        out_specs=vmem,
        scratch_shapes=[
            pltpu.VMEM((rows, tokens), bf16),
            pltpu.VMEM((2, rows, tokens), bf16),
            pltpu.VMEM((tokens, block), jnp.float32),
            pltpu.VMEM((tokens, width), bf16),
            pltpu.VMEM((units, width), bf16),
            pltpu.VMEM((units, width), bf16),
            pltpu.VMEM((units, width), bf16),
            pltpu.VMEM((4, rows, width // 4), bf16),
            pltpu.VMEM((4, rows, width // 4), bf16),
            pltpu.VMEM((rows, units), bf16),
            pltpu.VMEM((2, 4, rows, block), bf16),
            pltpu.VMEM((2, 4, rows, block), bf16),
            pltpu.VMEM((rows, block), bf16),
            pltpu.VMEM((rows, block), bf16),
            dma((7,)),
            dma((16,)), dma((16,)),
            dma((chunks, 2)), dma((chunks, 2)),
            dma((chunks, 4, 2, PIECES)), dma((chunks, 4, 2, PIECES)),
            dma((16,)), dma((16,)),
        ],
        compiler_params=pltpu.CompilerParams(
            collective_id=0, has_side_effects=True, vmem_limit_bytes=60 << 20
        ),
    )(
        expert_ids.T, gate_weights.T, hidden, jnp.swapaxes(w_gate, 1, 2),
        jnp.swapaxes(w_up, 1, 2), w_down,
    )


def solution(mesh):
    placed = (
        P(("dp", "context"), None),
        P(("dp", "context"), None),
        P(("dp", "context"), None),
        P("context", None, "tensor"),
        P("context", None, "tensor"),
        P("context", "tensor", None),
    )
    return jax.shard_map(
        local, mesh=mesh, in_specs=placed, out_specs=P(("dp", "context"), "tensor"), check_vma=False
    )
```

```python
import jax
import jax.numpy as jnp
from jax import lax
from jax.experimental import pallas as pl
from jax.experimental.pallas import tpu as pltpu
from jax.sharding import PartitionSpec as P

CAP = 32
CHIPS = 8
OFFSETS = (0, 2, 6, 4, 3, 5, 1, 7)
CHUNKS = ((0, 1, 8), (1, 2, 2), (3, 1, 2), (4, 2, 4), (6, 2, 8))
PIECES = 2
ORDER = (
    ("Y", 0), ("Y", 1), ("W",), ("Y", 2), ("Y", 3), ("Y", 4),
    ("A", 0), ("B", 0), ("S", 0, 0), ("S", 0, 1), ("S", 0, 2), ("A", 1),
    ("S", 0, 3), ("G", 1), ("A", 2), ("F", 0), ("B", 1), ("S", 1, 0),
    ("G", 2), ("S", 1, 1), ("B", 2), ("S", 2, 0), ("S", 1, 2), ("S", 2, 1),
    ("A", 3), ("S", 2, 2), ("S", 1, 3), ("B", 3), ("S", 3, 0), ("S", 2, 3),
    ("A", 4), ("B", 4), ("F", 1), ("S", 3, 1), ("S", 4, 0), ("F", 2),
    ("S", 3, 2), ("S", 4, 1), ("S", 3, 3), ("S", 4, 2), ("F", 3), ("S", 4, 3),
    ("F", 4), ("C", 0), ("C", 1), ("C", 2), ("C", 3), ("C", 4),
)
BOTH_LAST = (((1,), (1,)), ((), ()))
BOTH_FIRST = (((0,), (0,)), ((), ()))
MESH = pl.DeviceIdType.MESH


def kernel(
    ids_ref, mix_ref, hidden_ref, gate_ref, up_ref, down_ref, out_ref,
    sel_ref, comb_ref, total_ref, hid, wg, wu, wd, outgoing, arrived, act,
    rs_out, rs_in, mixed_rows, returned,
    load_sem, y_send, y_recv, f_send, f_recv, r_send, r_recv, b_send, b_recv,
):
    ctx, z = lax.axis_index("context"), lax.axis_index("tensor")
    y, core = ctx // 2, ctx % 2
    width = hidden_ref.shape[1]
    half, quarter, block = width // 2, width // 4, width // 8
    turn = (z // 2) % 2
    own = pl.multiple_of((z % 2) * half, half)
    other = pl.multiple_of((1 - z % 2) * half, half)
    right, left = (z + 1) % CHIPS, (z + CHIPS - 1) % CHIPS

    loads = []
    for n, (source, begin) in enumerate(((own, 0), (other, half))):
        loads.append(
            pltpu.make_async_copy(
                hidden_ref.at[:, pl.ds(source, half)], hid.at[:, pl.ds(begin, half)],
                load_sem.at[n],
            )
        )
    for n, (source, begin) in enumerate(((own, 0), (other, half))):
        for m, (src, dst) in enumerate(((gate_ref, wg), (up_ref, wu))):
            loads.append(
                pltpu.make_async_copy(
                    src.at[0, :, pl.ds(source, half)], dst.at[:, pl.ds(begin, half)],
                    load_sem.at[2 + 2 * n + m],
                )
            )
    loads.append(pltpu.make_async_copy(down_ref.at[0], wd, load_sem.at[6]))
    for load in loads:
        load.start()

    def peer(dy, dc):
        return ((y + dy) % CHIPS) * 2 + (core + dc) % 2

    barrier = pltpu.get_barrier_semaphore()
    for dy in range(CHIPS):
        for dc in range(2):
            if dy or dc:
                pl.semaphore_signal(
                    barrier, inc=1, device_id={"context": peer(dy, dc)}, device_id_type=MESH
                )
    for side in (right, left):
        pl.semaphore_signal(barrier, inc=1, device_id={"tensor": side}, device_id_type=MESH)

    tokens = hidden_ref.shape[0]
    row = lax.broadcasted_iota(jnp.int32, (2 * CHIPS, tokens), 0)
    place = row // 2
    shift = jnp.zeros_like(place)
    for n, offset in enumerate(OFFSETS):
        shift = jnp.where(place == n, offset, shift)
    expert = ((y + shift) % CHIPS) * 2 + (core + row % 2) % 2
    chosen = jnp.zeros((2 * CHIPS, tokens), jnp.float32)
    weight = jnp.zeros((2 * CHIPS, tokens), jnp.float32)
    for n in range(ids_ref.shape[0]):
        match = ids_ref[n:n + 1, :] == expert
        chosen = jnp.where(match, 1.0, chosen)
        weight = jnp.where(match, mix_ref[n:n + 1, :], weight)
    before = (
        lax.broadcasted_iota(jnp.int32, (tokens, tokens), 0)
        <= lax.broadcasted_iota(jnp.int32, (tokens, tokens), 1)
    )
    count = jnp.dot(
        chosen.astype(jnp.bfloat16), jnp.where(before, 1.0, 0.0).astype(jnp.bfloat16),
        preferred_element_type=jnp.float32,
    )
    slot = jnp.where(chosen > 0.0, count - 1.0, -1.0)
    slot_ids = lax.broadcasted_iota(jnp.int32, (CAP, tokens), 0).astype(jnp.float32)
    for n in range(2 * CHIPS):
        sel_ref[n * CAP:(n + 1) * CAP, :] = jnp.where(
            slot[n:n + 1, :] == slot_ids, 1.0, 0.0
        ).astype(jnp.bfloat16)

    loads[0].wait()
    loads[1].wait()
    pl.semaphore_wait(barrier, 2 * CHIPS + 1)

    y_copies, forwards, sums, backs = {}, {}, {}, {}

    def extent(k):
        begin, count, eighths = CHUNKS[k]
        return begin * 2 * CAP, (begin + count) * 2 * CAP, eighths // 2

    def dispatch(k):
        low, top, quarters = extent(k)
        for q in range(quarters):
            at = turn if quarters == 1 else q
            columns = pl.ds(pl.multiple_of(at * quarter, quarter), quarter)
            picked = jnp.dot(
                sel_ref[low:top, :], hid[:, columns],
                preferred_element_type=jnp.float32,
            ).astype(jnp.bfloat16)
            outgoing[at, low:top, :] = picked
            if low == 0:
                arrived[q, 0:CAP, :] = picked[0:CAP]
        for n in range(low // CAP, top // CAP):
            if n == 0:
                continue
            piece = (pl.ds(turn if quarters == 1 else 0, quarters), pl.ds(CAP * n, CAP), slice(None))
            copy = pltpu.make_async_remote_copy(
                src_ref=outgoing.at[piece], dst_ref=arrived.at[piece],
                send_sem=y_send.at[n], recv_sem=y_recv.at[n],
                device_id={"context": peer(OFFSETS[n // 2], n % 2)}, device_id_type=MESH,
            )
            copy.start()
            y_copies[n] = copy

    def weigh():
        for n in range(2 * CHIPS):
            combiner = jnp.where(slot[n:n + 1, :] == slot_ids, weight[n:n + 1, :], 0.0)
            high = combiner.astype(jnp.bfloat16)
            comb_ref[0, n * CAP:(n + 1) * CAP, :] = high
            comb_ref[1, n * CAP:(n + 1) * CAP, :] = (
                combiner - high.astype(jnp.float32)
            ).astype(jnp.bfloat16)

    def arrive(k):
        low, top, quarters = extent(k)
        for n in range(low // CAP, top // CAP):
            if n:
                y_copies[n].wait_recv()
        if quarters == 4:
            return
        span = pl.ds(low, top - low)
        for side, to in enumerate((right, left)):
            at = turn if quarters == 1 else side
            copy = pltpu.make_async_remote_copy(
                src_ref=arrived.at[at, span, :], dst_ref=arrived.at[2 + at, span, :],
                send_sem=f_send.at[k, side], recv_sem=f_recv.at[k, side],
                device_id={"tensor": to}, device_id_type=MESH,
            )
            copy.start()
            forwards[k, side] = copy

    def relay(k):
        low, top, _ = extent(k)
        for side, to in enumerate((right, left)):
            at = ((left if side == 0 else right) // 2) % 2
            forwards[k, side].wait_recv()
            place = (pl.ds(low, top - low), pl.ds(side * block, block))
            copy = pltpu.make_async_remote_copy(
                src_ref=arrived.at[(2 + at,) + place], dst_ref=arrived.at[(at,) + place],
                send_sem=f_send.at[k, 2 + side], recv_sem=f_recv.at[k, 2 + side],
                device_id={"tensor": to}, device_id_type=MESH,
            )
            copy.start()
            forwards[k, 2 + side] = copy

    def expand(k):
        low, top, quarters = extent(k)
        if quarters == 1:
            for side in range(2):
                forwards[k, 2 + side].wait_recv()
        if k == 0:
            for load in loads[2:]:
                load.wait()
        gate = up = None
        for q in range(4):
            if quarters == 2 and q >= 2:
                forwards[k, q - 2].wait_recv()
            x = arrived[q, low:top, :]
            here = slice(q * quarter, (q + 1) * quarter)
            g = lax.dot_general(x, wg[:, here], BOTH_LAST, preferred_element_type=jnp.float32)
            u = lax.dot_general(x, wu[:, here], BOTH_LAST, preferred_element_type=jnp.float32)
            gate = g if gate is None else gate + g
            up = u if up is None else up + u
        act[low:top, :] = (gate / (1.0 + jnp.exp(-gate)) * up).astype(jnp.bfloat16)

    def part(k, target, begin, size):
        low, top, _ = extent(k)
        columns = pl.ds(pl.multiple_of(target * block + begin, size), size)
        return jnp.dot(act[low:top, :], wd[:, columns], preferred_element_type=jnp.float32)

    narrow = block // 2

    def step(k, s):
        low, top, _ = extent(k)
        size = (top - low) // PIECES
        totals = []
        for side in range(2):
            shift = 4 - s
            target = (z + shift) % CHIPS if side == 0 else (z + CHIPS - shift) % CHIPS
            if s == 0:
                totals.append(part(k, target, side * narrow, narrow))
            else:
                totals.append(part(k, target, 0, block))
        for piece in range(PIECES):
            begin, end = low + piece * size, low + (piece + 1) * size
            for side, to in enumerate((right, left)):
                total = totals[side][piece * size:(piece + 1) * size]
                if s:
                    sums[k, s - 1, side, piece].wait_recv()
                if s == 0:
                    rs_out[side, 0, begin:end, 0:narrow] = total.astype(jnp.bfloat16)
                elif s == 1:
                    mine = slice(side * narrow, (side + 1) * narrow)
                    rest = slice((1 - side) * narrow, (2 - side) * narrow)
                    rs_out[side, s, begin:end, mine] = (
                        total[:, mine] + rs_in[side, 0, begin:end, 0:narrow].astype(jnp.float32)
                    ).astype(jnp.bfloat16)
                    rs_out[side, s, begin:end, rest] = total[:, rest].astype(jnp.bfloat16)
                else:
                    total = total + rs_in[side, s - 1, begin:end, :].astype(jnp.float32)
                    rs_out[side, s, begin:end, :] = total.astype(jnp.bfloat16)
                place = (side, s, pl.ds(begin, size), pl.ds(0, block if s else narrow))
                copy = pltpu.make_async_remote_copy(
                    src_ref=rs_out.at[place], dst_ref=rs_in.at[place],
                    send_sem=r_send.at[k, s, side, piece], recv_sem=r_recv.at[k, s, side, piece],
                    device_id={"tensor": to}, device_id_type=MESH,
                )
                copy.start()
                sums[k, s, side, piece] = copy

    def finish(k):
        low, top, _ = extent(k)
        size = (top - low) // PIECES
        whole = part(k, z, 0, block)
        for piece in range(PIECES):
            begin, end = low + piece * size, low + (piece + 1) * size
            total = whole[piece * size:(piece + 1) * size]
            for side in range(2):
                sums[k, 3, side, piece].wait_recv()
                total = total + rs_in[side, 3, begin:end, :].astype(jnp.float32)
            total = total.astype(jnp.bfloat16)
            mixed_rows[begin:end, :] = total
            for n in range(begin // CAP, end // CAP):
                if n == 0:
                    returned[0:CAP, :] = total[0:CAP]
                    continue
                span = pl.ds(CAP * n, CAP)
                copy = pltpu.make_async_remote_copy(
                    src_ref=mixed_rows.at[span, :], dst_ref=returned.at[span, :],
                    send_sem=b_send.at[n], recv_sem=b_recv.at[n],
                    device_id={"context": peer(CHIPS - OFFSETS[n // 2], n % 2)},
                    device_id_type=MESH,
                )
                copy.start()
                backs[n] = copy

    def combine(k):
        low, top, _ = extent(k)
        for n in range(low // CAP, top // CAP):
            if n:
                backs[n].wait_recv()
        total = None if k == 0 else total_ref[...]
        for n in range(2):
            term = lax.dot_general(
                comb_ref[n, low:top, :], returned[low:top, :], BOTH_FIRST,
                preferred_element_type=jnp.float32,
            )
            total = term if total is None else total + term
        if k == len(CHUNKS) - 1:
            out_ref[...] = total.astype(out_ref.dtype)
        else:
            total_ref[...] = total

    tasks = {
        "Y": dispatch, "A": arrive, "G": relay, "B": expand, "S": step, "F": finish,
        "C": combine, "W": weigh,
    }
    for task in ORDER:
        tasks[task[0]](*task[1:])

    for group in (y_copies, forwards, sums, backs):
        for copy in group.values():
            copy.wait_send()


def local(hidden, expert_ids, gate_weights, w_gate, w_up, w_down):
    tokens, width = hidden.shape
    units = w_gate.shape[2]
    block = width // CHIPS
    rows = 2 * CHIPS * CAP
    chunks = len(CHUNKS)
    bf16 = jnp.bfloat16
    vmem = pl.BlockSpec(memory_space=pltpu.VMEM)
    hbm = pl.BlockSpec(memory_space=pl.ANY)
    dma = pltpu.SemaphoreType.DMA
    return pl.pallas_call(
        kernel,
        out_shape=jax.ShapeDtypeStruct((tokens, block), bf16),
        in_specs=[vmem] * 2 + [hbm] * 4,
        out_specs=vmem,
        scratch_shapes=[
            pltpu.VMEM((rows, tokens), bf16),
            pltpu.VMEM((2, rows, tokens), bf16),
            pltpu.VMEM((tokens, block), jnp.float32),
            pltpu.VMEM((tokens, width), bf16),
            pltpu.VMEM((units, width), bf16),
            pltpu.VMEM((units, width), bf16),
            pltpu.VMEM((units, width), bf16),
            pltpu.VMEM((4, rows, width // 4), bf16),
            pltpu.VMEM((4, rows, width // 4), bf16),
            pltpu.VMEM((rows, units), bf16),
            pltpu.VMEM((2, 4, rows, block), bf16),
            pltpu.VMEM((2, 4, rows, block), bf16),
            pltpu.VMEM((rows, block), bf16),
            pltpu.VMEM((rows, block), bf16),
            dma((7,)),
            dma((16,)), dma((16,)),
            dma((chunks, 4)), dma((chunks, 4)),
            dma((chunks, 4, 2, PIECES)), dma((chunks, 4, 2, PIECES)),
            dma((16,)), dma((16,)),
        ],
        compiler_params=pltpu.CompilerParams(
            collective_id=0, has_side_effects=True, vmem_limit_bytes=60 << 20
        ),
    )(
        expert_ids.T, gate_weights.T, hidden, jnp.swapaxes(w_gate, 1, 2),
        jnp.swapaxes(w_up, 1, 2), w_down,
    )


def solution(mesh):
    placed = (
        P(("dp", "context"), None),
        P(("dp", "context"), None),
        P(("dp", "context"), None),
        P("context", None, "tensor"),
        P("context", None, "tensor"),
        P("context", "tensor", None),
    )
    return jax.shard_map(
        local, mesh=mesh, in_specs=placed, out_specs=P(("dp", "context"), "tensor"), check_vma=False
    )
```

```python
import jax
import jax.numpy as jnp
from jax import lax
from jax.experimental import pallas as pl
from jax.experimental.pallas import tpu as pltpu
from jax.sharding import PartitionSpec as P

CAP = 32
CHIPS = 8
OFFSETS = (0, 2, 6, 4, 3, 5, 1, 7)
CHUNKS = ((0, 1, 8), (1, 2, 2), (3, 1, 2), (4, 2, 4), (6, 2, 8))
PIECES = 2
ORDER = (
    ("Y", 1), ("Y", 0), ("A", 0), ("B", 0), ("D", 0), ("S", 0, 0),
    ("Y", 2), ("S", 0, 1), ("S", 0, 2), ("W",), ("A", 1), ("Y", 3),
    ("S", 0, 3), ("G", 1), ("A", 2), ("Y", 4), ("F", 0), ("B", 1),
    ("D", 1), ("S", 1, 0), ("G", 2), ("S", 1, 1), ("B", 2), ("D", 2),
    ("S", 2, 0), ("S", 1, 2), ("S", 2, 1), ("A", 3), ("S", 2, 2), ("S", 1, 3),
    ("B", 3), ("D", 3), ("S", 3, 0), ("S", 2, 3), ("A", 4), ("B", 4),
    ("D", 4), ("F", 1), ("S", 3, 1), ("S", 4, 0), ("F", 2), ("S", 3, 2),
    ("S", 4, 1), ("S", 3, 3), ("S", 4, 2), ("F", 3), ("S", 4, 3), ("F", 4),
    ("C", 0), ("C", 1), ("C", 2), ("C", 3), ("C", 4),
)
BOTH_LAST = (((1,), (1,)), ((), ()))
BOTH_FIRST = (((0,), (0,)), ((), ()))
MESH = pl.DeviceIdType.MESH


def kernel(
    ids_ref, mix_ref, hidden_ref, gate_ref, up_ref, down_ref, out_ref,
    sel_ref, comb_ref, total_ref, hid, wg, wu, wd, outgoing, arrived, act,
    rs_out, rs_in, mixed_rows, returned,
    load_sem, y_send, y_recv, f_send, f_recv, r_send, r_recv, b_send, b_recv,
):
    ctx, z = lax.axis_index("context"), lax.axis_index("tensor")
    y, core = ctx // 2, ctx % 2
    width = hidden_ref.shape[1]
    half, quarter, block = width // 2, width // 4, width // 8
    turn = (z // 2) % 2
    own = pl.multiple_of((z % 2) * half, half)
    other = pl.multiple_of((1 - z % 2) * half, half)
    right, left = (z + 1) % CHIPS, (z + CHIPS - 1) % CHIPS

    def peer(dy, dc):
        return ((y + dy) % CHIPS) * 2 + (core + dc) % 2

    barrier = pltpu.get_barrier_semaphore()
    for dy in range(CHIPS):
        for dc in range(2):
            if dy or dc:
                pl.semaphore_signal(
                    barrier, inc=1, device_id={"context": peer(dy, dc)}, device_id_type=MESH
                )
    for side in (right, left):
        pl.semaphore_signal(barrier, inc=1, device_id={"tensor": side}, device_id_type=MESH)

    loads = []
    for n, (source, begin) in enumerate(((own, 0), (other, half))):
        loads.append(
            pltpu.make_async_copy(
                hidden_ref.at[:, pl.ds(source, half)], hid.at[:, pl.ds(begin, half)],
                load_sem.at[n],
            )
        )
    for n, (source, begin) in enumerate(((own, 0), (other, half))):
        for m, (src, dst) in enumerate(((gate_ref, wg), (up_ref, wu))):
            loads.append(
                pltpu.make_async_copy(
                    src.at[0, :, pl.ds(source, half)], dst.at[:, pl.ds(begin, half)],
                    load_sem.at[2 + 2 * n + m],
                )
            )
    loads.append(pltpu.make_async_copy(down_ref.at[0], wd, load_sem.at[6]))
    for load in loads:
        load.start()

    tokens = hidden_ref.shape[0]
    row = lax.broadcasted_iota(jnp.int32, (2 * CHIPS, tokens), 0)
    place = row // 2
    shift = jnp.zeros_like(place)
    for n, offset in enumerate(OFFSETS):
        shift = jnp.where(place == n, offset, shift)
    expert = ((y + shift) % CHIPS) * 2 + (core + row % 2) % 2
    chosen = jnp.zeros((2 * CHIPS, tokens), jnp.float32)
    weight = jnp.zeros((2 * CHIPS, tokens), jnp.float32)
    for n in range(ids_ref.shape[0]):
        match = ids_ref[n:n + 1, :] == expert
        chosen = jnp.where(match, 1.0, chosen)
        weight = jnp.where(match, mix_ref[n:n + 1, :], weight)
    before = (
        lax.broadcasted_iota(jnp.int32, (tokens, tokens), 0)
        <= lax.broadcasted_iota(jnp.int32, (tokens, tokens), 1)
    )
    count = jnp.dot(
        chosen.astype(jnp.bfloat16), jnp.where(before, 1.0, 0.0).astype(jnp.bfloat16),
        preferred_element_type=jnp.float32,
    )
    slot = jnp.where(chosen > 0.0, count - 1.0, -1.0)
    slot_ids = lax.broadcasted_iota(jnp.int32, (CAP, tokens), 0).astype(jnp.float32)
    for n in range(2 * CHIPS):
        sel_ref[n * CAP:(n + 1) * CAP, :] = jnp.where(
            slot[n:n + 1, :] == slot_ids, 1.0, 0.0
        ).astype(jnp.bfloat16)

    loads[0].wait()
    loads[1].wait()
    pl.semaphore_wait(barrier, 2 * CHIPS + 1)

    y_copies, forwards, sums, backs = {}, {}, {}, {}

    def extent(k):
        begin, count, eighths = CHUNKS[k]
        return begin * 2 * CAP, (begin + count) * 2 * CAP, eighths // 2

    def dispatch(k):
        low, top, quarters = extent(k)
        for q in range(quarters):
            at = turn if quarters == 1 else q
            columns = pl.ds(pl.multiple_of(at * quarter, quarter), quarter)
            picked = jnp.dot(
                sel_ref[low:top, :], hid[:, columns],
                preferred_element_type=jnp.float32,
            ).astype(jnp.bfloat16)
            outgoing[at, low:top, :] = picked
            if low == 0:
                arrived[q, 0:CAP, :] = picked[0:CAP]
        for n in range(low // CAP, top // CAP):
            if n == 0:
                continue
            piece = (pl.ds(turn if quarters == 1 else 0, quarters), pl.ds(CAP * n, CAP), slice(None))
            copy = pltpu.make_async_remote_copy(
                src_ref=outgoing.at[piece], dst_ref=arrived.at[piece],
                send_sem=y_send.at[n], recv_sem=y_recv.at[n],
                device_id={"context": peer(OFFSETS[n // 2], n % 2)}, device_id_type=MESH,
            )
            copy.start()
            y_copies[n] = copy

    def weigh():
        for n in range(2 * CHIPS):
            combiner = jnp.where(slot[n:n + 1, :] == slot_ids, weight[n:n + 1, :], 0.0)
            high = combiner.astype(jnp.bfloat16)
            comb_ref[0, n * CAP:(n + 1) * CAP, :] = high
            comb_ref[1, n * CAP:(n + 1) * CAP, :] = (
                combiner - high.astype(jnp.float32)
            ).astype(jnp.bfloat16)

    def arrive(k):
        low, top, quarters = extent(k)
        for n in range(low // CAP, top // CAP):
            if n:
                y_copies[n].wait_recv()
        if quarters == 4:
            return
        span = pl.ds(low, top - low)
        for side, to in enumerate((right, left)):
            at = turn if quarters == 1 else side
            copy = pltpu.make_async_remote_copy(
                src_ref=arrived.at[at, span, :], dst_ref=arrived.at[2 + at, span, :],
                send_sem=f_send.at[k, side], recv_sem=f_recv.at[k, side],
                device_id={"tensor": to}, device_id_type=MESH,
            )
            copy.start()
            forwards[k, side] = copy

    def relay(k):
        low, top, _ = extent(k)
        for side, to in enumerate((right, left)):
            at = ((left if side == 0 else right) // 2) % 2
            forwards[k, side].wait_recv()
            place = (pl.ds(low, top - low), pl.ds(side * block, block))
            copy = pltpu.make_async_remote_copy(
                src_ref=arrived.at[(2 + at,) + place], dst_ref=arrived.at[(at,) + place],
                send_sem=f_send.at[k, 2 + side], recv_sem=f_recv.at[k, 2 + side],
                device_id={"tensor": to}, device_id_type=MESH,
            )
            copy.start()
            forwards[k, 2 + side] = copy

    halves = {}

    def multiply(k, quarters):
        low, top, _ = extent(k)
        for q in quarters:
            x = arrived[q, low:top, :]
            here = slice(q * quarter, (q + 1) * quarter)
            terms = [
                lax.dot_general(x, w[:, here], BOTH_LAST, preferred_element_type=jnp.float32)
                for w in (wg, wu)
            ]
            halves[k] = [a + b for a, b in zip(halves[k], terms)] if k in halves else terms

    def expand(k):
        if k == 0:
            for load in loads[2:]:
                load.wait()
        multiply(k, (2, 3) if extent(k)[2] == 1 else (0, 1))

    def activate(k):
        low, top, quarters = extent(k)
        if quarters < 4:
            for side in range(2):
                forwards[k, side + (2 if quarters == 1 else 0)].wait_recv()
        multiply(k, (0, 1) if quarters == 1 else (2, 3))
        gate, up = halves.pop(k)
        act[low:top, :] = (gate / (1.0 + jnp.exp(-gate)) * up).astype(jnp.bfloat16)

    def part(k, target, begin, size):
        low, top, _ = extent(k)
        columns = pl.ds(pl.multiple_of(target * block + begin, size), size)
        return jnp.dot(act[low:top, :], wd[:, columns], preferred_element_type=jnp.float32)

    narrow = block // 2

    def step(k, s):
        low, top, _ = extent(k)
        size = (top - low) // PIECES
        totals = []
        for side in range(2):
            shift = 4 - s
            target = (z + shift) % CHIPS if side == 0 else (z + CHIPS - shift) % CHIPS
            if s == 0:
                totals.append(part(k, target, side * narrow, narrow))
            else:
                totals.append(part(k, target, 0, block))
        for piece in range(PIECES):
            begin, end = low + piece * size, low + (piece + 1) * size
            for side, to in enumerate((right, left)):
                total = totals[side][piece * size:(piece + 1) * size]
                if s:
                    sums[k, s - 1, side, piece].wait_recv()
                if s == 0:
                    rs_out[side, 0, begin:end, 0:narrow] = total.astype(jnp.bfloat16)
                elif s == 1:
                    mine = slice(side * narrow, (side + 1) * narrow)
                    rest = slice((1 - side) * narrow, (2 - side) * narrow)
                    rs_out[side, s, begin:end, mine] = (
                        total[:, mine] + rs_in[side, 0, begin:end, 0:narrow].astype(jnp.float32)
                    ).astype(jnp.bfloat16)
                    rs_out[side, s, begin:end, rest] = total[:, rest].astype(jnp.bfloat16)
                else:
                    total = total + rs_in[side, s - 1, begin:end, :].astype(jnp.float32)
                    rs_out[side, s, begin:end, :] = total.astype(jnp.bfloat16)
                place = (side, s, pl.ds(begin, size), pl.ds(0, block if s else narrow))
                copy = pltpu.make_async_remote_copy(
                    src_ref=rs_out.at[place], dst_ref=rs_in.at[place],
                    send_sem=r_send.at[k, s, side, piece], recv_sem=r_recv.at[k, s, side, piece],
                    device_id={"tensor": to}, device_id_type=MESH,
                )
                copy.start()
                sums[k, s, side, piece] = copy

    def finish(k):
        low, top, _ = extent(k)
        size = (top - low) // PIECES
        whole = part(k, z, 0, block)
        for piece in range(PIECES):
            begin, end = low + piece * size, low + (piece + 1) * size
            total = whole[piece * size:(piece + 1) * size]
            for side in range(2):
                sums[k, 3, side, piece].wait_recv()
                total = total + rs_in[side, 3, begin:end, :].astype(jnp.float32)
            total = total.astype(jnp.bfloat16)
            mixed_rows[begin:end, :] = total
            for n in range(begin // CAP, end // CAP):
                if n == 0:
                    returned[0:CAP, :] = total[0:CAP]
                    continue
                span = pl.ds(CAP * n, CAP)
                copy = pltpu.make_async_remote_copy(
                    src_ref=mixed_rows.at[span, :], dst_ref=returned.at[span, :],
                    send_sem=b_send.at[n], recv_sem=b_recv.at[n],
                    device_id={"context": peer(CHIPS - OFFSETS[n // 2], n % 2)},
                    device_id_type=MESH,
                )
                copy.start()
                backs[n] = copy

    def combine(k):
        low, top, _ = extent(k)
        for n in range(low // CAP, top // CAP):
            if n:
                backs[n].wait_recv()
        total = None if k == 0 else total_ref[...]
        for n in range(2):
            term = lax.dot_general(
                comb_ref[n, low:top, :], returned[low:top, :], BOTH_FIRST,
                preferred_element_type=jnp.float32,
            )
            total = term if total is None else total + term
        if k == len(CHUNKS) - 1:
            out_ref[...] = total.astype(out_ref.dtype)
        else:
            total_ref[...] = total

    tasks = {
        "Y": dispatch, "A": arrive, "G": relay, "B": expand, "D": activate, "S": step, "F": finish,
        "C": combine, "W": weigh,
    }
    for task in ORDER:
        tasks[task[0]](*task[1:])

    for group in (y_copies, forwards, sums, backs):
        for copy in group.values():
            copy.wait_send()


def local(hidden, expert_ids, gate_weights, w_gate, w_up, w_down):
    tokens, width = hidden.shape
    units = w_gate.shape[2]
    block = width // CHIPS
    rows = 2 * CHIPS * CAP
    chunks = len(CHUNKS)
    bf16 = jnp.bfloat16
    vmem = pl.BlockSpec(memory_space=pltpu.VMEM)
    hbm = pl.BlockSpec(memory_space=pl.ANY)
    dma = pltpu.SemaphoreType.DMA
    return pl.pallas_call(
        kernel,
        out_shape=jax.ShapeDtypeStruct((tokens, block), bf16),
        in_specs=[vmem] * 2 + [hbm] * 4,
        out_specs=vmem,
        scratch_shapes=[
            pltpu.VMEM((rows, tokens), bf16),
            pltpu.VMEM((2, rows, tokens), bf16),
            pltpu.VMEM((tokens, block), jnp.float32),
            pltpu.VMEM((tokens, width), bf16),
            pltpu.VMEM((units, width), bf16),
            pltpu.VMEM((units, width), bf16),
            pltpu.VMEM((units, width), bf16),
            pltpu.VMEM((4, rows, width // 4), bf16),
            pltpu.VMEM((4, rows, width // 4), bf16),
            pltpu.VMEM((rows, units), bf16),
            pltpu.VMEM((2, 4, rows, block), bf16),
            pltpu.VMEM((2, 4, rows, block), bf16),
            pltpu.VMEM((rows, block), bf16),
            pltpu.VMEM((rows, block), bf16),
            dma((7,)),
            dma((16,)), dma((16,)),
            dma((chunks, 4)), dma((chunks, 4)),
            dma((chunks, 4, 2, PIECES)), dma((chunks, 4, 2, PIECES)),
            dma((16,)), dma((16,)),
        ],
        compiler_params=pltpu.CompilerParams(
            collective_id=0, has_side_effects=True, vmem_limit_bytes=60 << 20
        ),
    )(
        expert_ids.T, gate_weights.T, hidden, jnp.swapaxes(w_gate, 1, 2),
        jnp.swapaxes(w_up, 1, 2), w_down,
    )


def solution(mesh):
    placed = (
        P(("dp", "context"), None),
        P(("dp", "context"), None),
        P(("dp", "context"), None),
        P("context", None, "tensor"),
        P("context", None, "tensor"),
        P("context", "tensor", None),
    )
    return jax.shard_map(
        local, mesh=mesh, in_specs=placed, out_specs=P(("dp", "context"), "tensor"), check_vma=False
    )
```

```python
import jax
import jax.numpy as jnp
from jax import lax
from jax.experimental import pallas as pl
from jax.experimental.pallas import tpu as pltpu
from jax.sharding import PartitionSpec as P

CAP = 32
CHIPS = 8
OFFSETS = (0, 2, 6, 4, 3, 5, 1, 7)
CHUNKS = ((0, 1, 8), (1, 2, 2), (3, 1, 2), (4, 2, 4), (6, 2, 8))
PIECES = 2
ORDER = (
    ("Y", 1), ("Y", 0), ("A", 0), ("B", 0), ("D", 0), ("S", 0, 0),
    ("Y", 2), ("S", 0, 1), ("S", 0, 2), ("W",), ("A", 1), ("Y", 3),
    ("S", 0, 3), ("G", 1), ("A", 2), ("Y", 4), ("F", 0), ("B", 1),
    ("D", 1), ("S", 1, 0), ("G", 2), ("S", 1, 1), ("B", 2), ("D", 2),
    ("S", 2, 0), ("S", 1, 2), ("S", 2, 1), ("A", 3), ("S", 2, 2), ("S", 1, 3),
    ("B", 3), ("D", 3), ("S", 3, 0), ("S", 2, 3), ("A", 4), ("B", 4),
    ("D", 4), ("F", 1), ("S", 3, 1), ("S", 4, 0), ("F", 2), ("S", 3, 2),
    ("S", 4, 1), ("S", 3, 3), ("S", 4, 2), ("F", 3), ("S", 4, 3), ("F", 4),
    ("C", 0), ("C", 1), ("C", 2), ("C", 3), ("C", 4),
)
BOTH_LAST = (((1,), (1,)), ((), ()))
BOTH_FIRST = (((0,), (0,)), ((), ()))
MESH = pl.DeviceIdType.MESH


def kernel(
    ids_ref, mix_ref, hidden_ref, gate_ref, up_ref, down_ref, out_ref,
    sel_ref, comb_ref, total_ref, hid, pair, wd, outgoing, arrived, act,
    rs_out, rs_in, mixed_rows, returned,
    load_sem, y_send, y_recv, f_send, f_recv, r_send, r_recv, b_send, b_recv,
):
    ctx, z = lax.axis_index("context"), lax.axis_index("tensor")
    y, core = ctx // 2, ctx % 2
    width, units = hidden_ref.shape[1], gate_ref.shape[1]
    half, quarter, block = width // 2, width // 4, width // 8
    turn = (z // 2) % 2
    own = pl.multiple_of((z % 2) * half, half)
    other = pl.multiple_of((1 - z % 2) * half, half)
    right, left = (z + 1) % CHIPS, (z + CHIPS - 1) % CHIPS

    def peer(dy, dc):
        return ((y + dy) % CHIPS) * 2 + (core + dc) % 2

    barrier = pltpu.get_barrier_semaphore()
    for dy in range(CHIPS):
        for dc in range(2):
            if dy or dc:
                pl.semaphore_signal(
                    barrier, inc=1, device_id={"context": peer(dy, dc)}, device_id_type=MESH
                )
    for side in (right, left):
        pl.semaphore_signal(barrier, inc=1, device_id={"tensor": side}, device_id_type=MESH)

    loads = []
    for n, (source, begin) in enumerate(((own, 0), (other, half))):
        loads.append(
            pltpu.make_async_copy(
                hidden_ref.at[:, pl.ds(source, half)], hid.at[:, pl.ds(begin, half)],
                load_sem.at[n],
            )
        )
    for n, (source, begin) in enumerate(((own, 0), (other, half))):
        for m, src in enumerate((gate_ref, up_ref)):
            loads.append(
                pltpu.make_async_copy(
                    src.at[0, :, pl.ds(source, half)],
                    pair.at[pl.ds(m * units, units), pl.ds(begin, half)],
                    load_sem.at[2 + 2 * n + m],
                )
            )
    loads.append(pltpu.make_async_copy(down_ref.at[0], wd, load_sem.at[6]))
    for load in loads:
        load.start()

    tokens = hidden_ref.shape[0]
    row = lax.broadcasted_iota(jnp.int32, (2 * CHIPS, tokens), 0)
    place = row // 2
    shift = jnp.zeros_like(place)
    for n, offset in enumerate(OFFSETS):
        shift = jnp.where(place == n, offset, shift)
    expert = ((y + shift) % CHIPS) * 2 + (core + row % 2) % 2
    chosen = jnp.zeros((2 * CHIPS, tokens), jnp.float32)
    weight = jnp.zeros((2 * CHIPS, tokens), jnp.float32)
    for n in range(ids_ref.shape[0]):
        match = ids_ref[n:n + 1, :] == expert
        chosen = jnp.where(match, 1.0, chosen)
        weight = jnp.where(match, mix_ref[n:n + 1, :], weight)
    before = (
        lax.broadcasted_iota(jnp.int32, (tokens, tokens), 0)
        <= lax.broadcasted_iota(jnp.int32, (tokens, tokens), 1)
    )
    count = jnp.dot(
        chosen.astype(jnp.bfloat16), jnp.where(before, 1.0, 0.0).astype(jnp.bfloat16),
        preferred_element_type=jnp.float32,
    )
    slot = jnp.where(chosen > 0.0, count - 1.0, -1.0)
    slot_ids = lax.broadcasted_iota(jnp.int32, (CAP, tokens), 0).astype(jnp.float32)
    for n in range(2 * CHIPS):
        sel_ref[n * CAP:(n + 1) * CAP, :] = jnp.where(
            slot[n:n + 1, :] == slot_ids, 1.0, 0.0
        ).astype(jnp.bfloat16)

    loads[0].wait()
    loads[1].wait()
    pl.semaphore_wait(barrier, 2 * CHIPS + 1)

    y_copies, forwards, sums, backs = {}, {}, {}, {}

    def extent(k):
        begin, count, eighths = CHUNKS[k]
        return begin * 2 * CAP, (begin + count) * 2 * CAP, eighths // 2

    def dispatch(k):
        low, top, quarters = extent(k)
        for q in range(quarters):
            at = turn if quarters == 1 else q
            columns = pl.ds(pl.multiple_of(at * quarter, quarter), quarter)
            picked = jnp.dot(
                sel_ref[low:top, :], hid[:, columns],
                preferred_element_type=jnp.float32,
            ).astype(jnp.bfloat16)
            outgoing[at, low:top, :] = picked
            if low == 0:
                arrived[q, 0:CAP, :] = picked[0:CAP]
        for n in range(low // CAP, top // CAP):
            if n == 0:
                continue
            piece = (pl.ds(turn if quarters == 1 else 0, quarters), pl.ds(CAP * n, CAP), slice(None))
            copy = pltpu.make_async_remote_copy(
                src_ref=outgoing.at[piece], dst_ref=arrived.at[piece],
                send_sem=y_send.at[n], recv_sem=y_recv.at[n],
                device_id={"context": peer(OFFSETS[n // 2], n % 2)}, device_id_type=MESH,
            )
            copy.start()
            y_copies[n] = copy

    def weigh():
        for n in range(2 * CHIPS):
            combiner = jnp.where(slot[n:n + 1, :] == slot_ids, weight[n:n + 1, :], 0.0)
            high = combiner.astype(jnp.bfloat16)
            comb_ref[0, n * CAP:(n + 1) * CAP, :] = high
            comb_ref[1, n * CAP:(n + 1) * CAP, :] = (
                combiner - high.astype(jnp.float32)
            ).astype(jnp.bfloat16)

    def arrive(k):
        low, top, quarters = extent(k)
        for n in range(low // CAP, top // CAP):
            if n:
                y_copies[n].wait_recv()
        if quarters == 4:
            return
        span = pl.ds(low, top - low)
        for side, to in enumerate((right, left)):
            at = turn if quarters == 1 else side
            copy = pltpu.make_async_remote_copy(
                src_ref=arrived.at[at, span, :], dst_ref=arrived.at[2 + at, span, :],
                send_sem=f_send.at[k, side], recv_sem=f_recv.at[k, side],
                device_id={"tensor": to}, device_id_type=MESH,
            )
            copy.start()
            forwards[k, side] = copy

    def relay(k):
        low, top, _ = extent(k)
        for side, to in enumerate((right, left)):
            at = ((left if side == 0 else right) // 2) % 2
            forwards[k, side].wait_recv()
            place = (pl.ds(low, top - low), pl.ds(side * block, block))
            copy = pltpu.make_async_remote_copy(
                src_ref=arrived.at[(2 + at,) + place], dst_ref=arrived.at[(at,) + place],
                send_sem=f_send.at[k, 2 + side], recv_sem=f_recv.at[k, 2 + side],
                device_id={"tensor": to}, device_id_type=MESH,
            )
            copy.start()
            forwards[k, 2 + side] = copy

    halves = {}

    def multiply(k, quarters):
        low, top, _ = extent(k)
        for q in quarters:
            x = arrived[q, low:top, :]
            here = slice(q * quarter, (q + 1) * quarter)
            term = lax.dot_general(
                x, pair[:, here], BOTH_LAST, preferred_element_type=jnp.float32
            )
            halves[k] = halves[k] + term if k in halves else term

    def expand(k):
        if k == 0:
            for load in loads[2:]:
                load.wait()
        multiply(k, (2, 3) if extent(k)[2] == 1 else (0, 1))

    def activate(k):
        low, top, quarters = extent(k)
        if quarters < 4:
            for side in range(2):
                forwards[k, side + (2 if quarters == 1 else 0)].wait_recv()
        multiply(k, (0, 1) if quarters == 1 else (2, 3))
        total = halves.pop(k)
        gate, up = total[:, 0:units], total[:, units:2 * units]
        act[low:top, :] = (gate / (1.0 + jnp.exp(-gate)) * up).astype(jnp.bfloat16)

    def part(k, target, begin, size):
        low, top, _ = extent(k)
        columns = pl.ds(pl.multiple_of(target * block + begin, size), size)
        return jnp.dot(act[low:top, :], wd[:, columns], preferred_element_type=jnp.float32)

    narrow = block // 2

    def step(k, s):
        low, top, _ = extent(k)
        size = (top - low) // PIECES
        totals = []
        for side in range(2):
            shift = 4 - s
            target = (z + shift) % CHIPS if side == 0 else (z + CHIPS - shift) % CHIPS
            if s == 0:
                totals.append(part(k, target, side * narrow, narrow))
            else:
                totals.append(part(k, target, 0, block))
        for piece in range(PIECES):
            begin, end = low + piece * size, low + (piece + 1) * size
            for side, to in enumerate((right, left)):
                total = totals[side][piece * size:(piece + 1) * size]
                if s:
                    sums[k, s - 1, side, piece].wait_recv()
                if s == 0:
                    rs_out[side, 0, begin:end, 0:narrow] = total.astype(jnp.bfloat16)
                elif s == 1:
                    mine = slice(side * narrow, (side + 1) * narrow)
                    rest = slice((1 - side) * narrow, (2 - side) * narrow)
                    rs_out[side, s, begin:end, mine] = (
                        total[:, mine] + rs_in[side, 0, begin:end, 0:narrow].astype(jnp.float32)
                    ).astype(jnp.bfloat16)
                    rs_out[side, s, begin:end, rest] = total[:, rest].astype(jnp.bfloat16)
                else:
                    total = total + rs_in[side, s - 1, begin:end, :].astype(jnp.float32)
                    rs_out[side, s, begin:end, :] = total.astype(jnp.bfloat16)
                place = (side, s, pl.ds(begin, size), pl.ds(0, block if s else narrow))
                copy = pltpu.make_async_remote_copy(
                    src_ref=rs_out.at[place], dst_ref=rs_in.at[place],
                    send_sem=r_send.at[k, s, side, piece], recv_sem=r_recv.at[k, s, side, piece],
                    device_id={"tensor": to}, device_id_type=MESH,
                )
                copy.start()
                sums[k, s, side, piece] = copy

    def finish(k):
        low, top, _ = extent(k)
        size = (top - low) // PIECES
        whole = part(k, z, 0, block)
        for piece in range(PIECES):
            begin, end = low + piece * size, low + (piece + 1) * size
            total = whole[piece * size:(piece + 1) * size]
            for side in range(2):
                sums[k, 3, side, piece].wait_recv()
                total = total + rs_in[side, 3, begin:end, :].astype(jnp.float32)
            total = total.astype(jnp.bfloat16)
            mixed_rows[begin:end, :] = total
            for n in range(begin // CAP, end // CAP):
                if n == 0:
                    returned[0:CAP, :] = total[0:CAP]
                    continue
                span = pl.ds(CAP * n, CAP)
                copy = pltpu.make_async_remote_copy(
                    src_ref=mixed_rows.at[span, :], dst_ref=returned.at[span, :],
                    send_sem=b_send.at[n], recv_sem=b_recv.at[n],
                    device_id={"context": peer(CHIPS - OFFSETS[n // 2], n % 2)},
                    device_id_type=MESH,
                )
                copy.start()
                backs[n] = copy

    def combine(k):
        low, top, _ = extent(k)
        for n in range(low // CAP, top // CAP):
            if n:
                backs[n].wait_recv()
        total = None if k == 0 else total_ref[...]
        for n in range(2):
            term = lax.dot_general(
                comb_ref[n, low:top, :], returned[low:top, :], BOTH_FIRST,
                preferred_element_type=jnp.float32,
            )
            total = term if total is None else total + term
        if k == len(CHUNKS) - 1:
            out_ref[...] = total.astype(out_ref.dtype)
        else:
            total_ref[...] = total

    tasks = {
        "Y": dispatch, "A": arrive, "G": relay, "B": expand, "D": activate, "S": step, "F": finish,
        "C": combine, "W": weigh,
    }
    for task in ORDER:
        tasks[task[0]](*task[1:])

    for group in (y_copies, forwards, sums, backs):
        for copy in group.values():
            copy.wait_send()


def local(hidden, expert_ids, gate_weights, w_gate, w_up, w_down):
    tokens, width = hidden.shape
    units = w_gate.shape[2]
    block = width // CHIPS
    rows = 2 * CHIPS * CAP
    chunks = len(CHUNKS)
    bf16 = jnp.bfloat16
    vmem = pl.BlockSpec(memory_space=pltpu.VMEM)
    hbm = pl.BlockSpec(memory_space=pl.ANY)
    dma = pltpu.SemaphoreType.DMA
    return pl.pallas_call(
        kernel,
        out_shape=jax.ShapeDtypeStruct((tokens, block), bf16),
        in_specs=[vmem] * 2 + [hbm] * 4,
        out_specs=vmem,
        scratch_shapes=[
            pltpu.VMEM((rows, tokens), bf16),
            pltpu.VMEM((2, rows, tokens), bf16),
            pltpu.VMEM((tokens, block), jnp.float32),
            pltpu.VMEM((tokens, width), bf16),
            pltpu.VMEM((2 * units, width), bf16),
            pltpu.VMEM((units, width), bf16),
            pltpu.VMEM((4, rows, width // 4), bf16),
            pltpu.VMEM((4, rows, width // 4), bf16),
            pltpu.VMEM((rows, units), bf16),
            pltpu.VMEM((2, 4, rows, block), bf16),
            pltpu.VMEM((2, 4, rows, block), bf16),
            pltpu.VMEM((rows, block), bf16),
            pltpu.VMEM((rows, block), bf16),
            dma((7,)),
            dma((16,)), dma((16,)),
            dma((chunks, 4)), dma((chunks, 4)),
            dma((chunks, 4, 2, PIECES)), dma((chunks, 4, 2, PIECES)),
            dma((16,)), dma((16,)),
        ],
        compiler_params=pltpu.CompilerParams(
            collective_id=0, has_side_effects=True, vmem_limit_bytes=60 << 20
        ),
    )(
        expert_ids.T, gate_weights.T, hidden, jnp.swapaxes(w_gate, 1, 2),
        jnp.swapaxes(w_up, 1, 2), w_down,
    )


def solution(mesh):
    placed = (
        P(("dp", "context"), None),
        P(("dp", "context"), None),
        P(("dp", "context"), None),
        P("context", None, "tensor"),
        P("context", None, "tensor"),
        P("context", "tensor", None),
    )
    return jax.shard_map(
        local, mesh=mesh, in_specs=placed, out_specs=P(("dp", "context"), "tensor"), check_vma=False
    )
```
